32 devices in a mesh: rows: 16 (over z, y, x), grp: 2 (over core).
Axes of the slice: x: 2, y: 2, z: 4, core: 2. Of those that a mesh axis runs over, the one named last changes fastest.
Arguments:
- snap_early: float32 [3072, 128, 128], P(('rows', 'grp')), as said below
- snap_late: float32 [3072, 128, 128], P(('rows', 'grp')), as said below
- block_ids: int32 [3072], P(('rows', 'grp')), may hold values from 0 to 3071, as said below
- block_owner: int32 [3072], replicated, may hold values from 0 to 31, as said below
- block_slot: int32 [3072], replicated, may hold values from 0 to 127, as said below
Outputs:
- modes: float32 [4096, 128, 128], P(('rows', 'grp'))
- operator: float32 [128, 128], replicated
The draws below stay inside these ranges and needn't reach their ends.
Inputs may be any that keep to these rules, and one draw needn't show every extreme that they name: block_ids is a permutation of 0 to 3071. `block_owner`: each analysis device owns at most 128 blocks and one owns exactly 128; among the blocks of one solver device (aligned runs of 96 slots of block_ids) at most 4 go to one analysis device, and in every draw some solver device sends exactly 4 to one. `block_slot`: the blocks of one analysis device take the slots 0 to c - 1, each once, where c is their count. `snap_early`: Real-valued snapshots with magnitudes from below one to some thousands, row and column scales spread by up to a factor of about 900; the matrix of all rows has full column rank. `snap_late`: Real-valued snapshots, the early ones advanced by one step of a linear flow plus noise.
All inputs are finite; a program needn't handle non-finite values.
Results may differ from the reference program's by a relative error of at most 0.0003.
Values sent between devices are 32-bit elements; how exact they have to be, the bound alone decides.
A program may use at most 128 MiB of HBM per device.

```python
import math
import jax
import jax.numpy as jnp
from jax import lax

K = 128
BLOCK = 128
SB_DEV = 96
CAP = 128
NBLOCKS = 3072
SLOTS_ALL = 4096


def snapshot_pair(key):
    keys = jax.random.split(jax.random.fold_in(key, 7), 7)
    row_total = NBLOCKS * BLOCK
    members = NBLOCKS // SB_DEV
    spread = math.log(10.0)
    normal_part = jax.random.normal(keys[0], (row_total, K), jnp.float32)
    mixing = jnp.eye(K, dtype=jnp.float32) + 0.3 * jax.random.normal(keys[1], (K, K), jnp.float32) / math.sqrt(K)
    column_scale = jnp.exp(jax.random.uniform(keys[2], (K,), jnp.float32, 0.0, math.log(10.0)))
    device_rank = (jnp.arange(row_total) // (SB_DEV * BLOCK)).astype(jnp.float32)
    ramp = 1.0 + 2.0 * device_rank / max(members - 1, 1)
    row_scale = jnp.exp(jax.random.uniform(keys[3], (row_total,), jnp.float32, 0.0, spread)) * ramp
    early_rows = row_scale[:, None] * jnp.dot(normal_part, mixing, precision=lax.Precision.HIGHEST) * column_scale[None, :]
    dynamics = 0.8 * jnp.eye(K, dtype=jnp.float32) + 0.5 * jax.random.normal(keys[5], (K, K), jnp.float32) / math.sqrt(K)
    noise = jax.random.normal(keys[6], (row_total, K), jnp.float32) * (0.3 * row_scale)[:, None] * column_scale[None, :]
    late_rows = jnp.dot(early_rows, dynamics, precision=lax.Precision.HIGHEST) + noise
    return (early_rows.reshape((NBLOCKS, BLOCK, K)), late_rows.reshape((NBLOCKS, BLOCK, K)))


def block_routing(key):
    keys = jax.random.split(jax.random.fold_in(key, 11), 3)
    members = NBLOCKS // SB_DEV
    spread = CAP - SB_DEV
    halves = members // 2
    order = jax.random.permutation(keys[0], members).astype(jnp.int32)
    deltas = jax.random.randint(keys[1], (halves,), 0, spread + 1).astype(jnp.int32).at[0].set(spread)
    counts = jnp.full((members,), SB_DEV, jnp.int32)
    counts = counts.at[order[:halves]].add(deltas).at[order[halves:2 * halves]].add(-deltas)
    ends = jnp.cumsum(counts).astype(jnp.int32)
    position = jnp.arange(NBLOCKS, dtype=jnp.int32)
    owner_at = jnp.sum((position[:, None] >= ends[None, :]).astype(jnp.int32), axis=1).astype(jnp.int32)
    starts = ends - counts
    slot_at = (position - starts[owner_at]).astype(jnp.int32)
    solver_slot = (position % members * SB_DEV + position // members).astype(jnp.int32)
    labels = jax.random.permutation(keys[2], NBLOCKS).astype(jnp.int32)
    identity_map = jnp.zeros((NBLOCKS,), jnp.int32).at[solver_slot].set(labels)
    owners = jnp.zeros((NBLOCKS,), jnp.int32).at[labels].set(owner_at)
    slots = jnp.zeros((NBLOCKS,), jnp.int32).at[labels].set(slot_at)
    return (identity_map, owners, slots)


def draw_snap_early(key, part):
    return snapshot_pair(key)[0]


def draw_snap_late(key, part):
    return snapshot_pair(key)[1]


def draw_block_ids(key, part):
    return block_routing(key)[0]


def draw_block_owner(key, part):
    return block_routing(key)[1]


def draw_block_slot(key, part):
    return block_routing(key)[2]


def setup_inputs(seed: int = 0) -> dict:
    streams_of = jax.random.split(jax.random.key(seed), 6)
    return {
        "snap_early": draw_snap_early(jax.random.fold_in(streams_of[5], 71), 0),
        "snap_late": draw_snap_late(jax.random.fold_in(streams_of[5], 71), 0),
        "block_ids": draw_block_ids(jax.random.fold_in(streams_of[5], 71), 0),
        "block_owner": draw_block_owner(jax.random.fold_in(streams_of[5], 71), 0),
        "block_slot": draw_block_slot(jax.random.fold_in(streams_of[5], 71), 0),
    }


def upper_factor(gram_total):
    order = gram_total.shape[0]
    index = jnp.arange(order, dtype=jnp.int32)

    def step(j, factor):
        column = lax.dynamic_slice_in_dim(factor, j, 1, 1)[:, 0]
        grow = lax.dynamic_slice_in_dim(gram_total, j, 1, 0)[0]
        rest = grow - jnp.dot(column, factor, precision=lax.Precision.HIGHEST)
        pivot = jnp.sqrt(jnp.sum(jnp.where(index == j, rest, 0.0)))
        newrow = jnp.where(index >= j, rest / pivot, 0.0)
        picked = (index == j).astype(gram_total.dtype)
        return factor + picked[:, None] * newrow[None, :]
    return lax.fori_loop(0, order, step, jnp.zeros_like(gram_total))

def upper_inverse(factor):
    order = factor.shape[0]
    index = jnp.arange(order, dtype=jnp.int32)

    def step(t, inverse):
        i = order - 1 - t
        frow = lax.dynamic_slice_in_dim(factor, i, 1, 0)[0]
        unit = (index == i).astype(factor.dtype)
        diagonal = jnp.sum(frow * unit)
        newrow = (unit - jnp.dot(frow, inverse, precision=lax.Precision.HIGHEST)) / diagonal
        return inverse + unit[:, None] * newrow[None, :]
    return lax.fori_loop(0, order, step, jnp.zeros_like(factor))

def reference(snap_early, snap_late, block_ids, block_owner, block_slot):
    row_total = snap_early.shape[0] * snap_early.shape[1]
    early_rows = snap_early.reshape((row_total, snap_early.shape[2]))
    late_rows = snap_late.reshape((row_total, snap_late.shape[2]))
    gram_total = jnp.einsum('rk,rl->kl', early_rows, early_rows, precision=lax.Precision.HIGHEST) / row_total
    cross_total = jnp.einsum('rk,rl->kl', early_rows, late_rows, precision=lax.Precision.HIGHEST) / row_total
    factor = upper_factor(gram_total)
    inverse = upper_inverse(factor)
    coupled = jnp.dot(cross_total, inverse, precision=lax.Precision.HIGHEST)
    operator = jnp.dot(inverse.T, coupled, precision=lax.Precision.HIGHEST)
    solved = jnp.dot(late_rows, inverse, precision=lax.Precision.HIGHEST)
    mode_blocks = solved.reshape(snap_late.shape)
    position = (block_owner[block_ids] * CAP + block_slot[block_ids]).astype(jnp.int32)
    output = jnp.zeros((SLOTS_ALL, snap_late.shape[1], snap_late.shape[2]), mode_blocks.dtype)
    output = output.at[position].set(mode_blocks)
    return (output, operator)
```

```python
import functools
import math

import jax
import jax.numpy as jnp
from jax import lax
from jax.experimental import pallas as pl
from jax.experimental.pallas import tpu as pltpu
from jax.sharding import PartitionSpec as P

CAP = 128
LANES = 128
TILE = 8
MESH = pl.DeviceIdType.MESH
HIGHEST = lax.Precision.HIGHEST


def arrange_kernel(place_ref, late_ref, payload_ref, sem):
    blocks = late_ref.shape[0]

    def send(i, carry):
        pltpu.make_async_copy(late_ref.at[i], payload_ref.at[place_ref[i]], sem).start()
        return carry

    lax.fori_loop(0, blocks, send, 0)
    pltpu.make_async_copy(late_ref, payload_ref.at[pl.ds(0, blocks)], sem).wait()


def arrange(place, late, slots):
    return pl.pallas_call(
        arrange_kernel,
        out_shape=jax.ShapeDtypeStruct((slots,) + late.shape[1:], late.dtype),
        in_specs=[
            pl.BlockSpec(memory_space=pltpu.SMEM),
            pl.BlockSpec(memory_space=pl.ANY),
        ],
        out_specs=pl.BlockSpec(memory_space=pl.ANY),
        scratch_shapes=[pltpu.SemaphoreType.DMA],
        compiler_params=pltpu.CompilerParams(has_side_effects=True),
    )(place, late)


def exchange_kernel(
    members, cores, per_peer, chunk, first, second, row_total,
    early_ref, late_ref, payload_ref, table_ref,
    arrived_ref, inverse_ref, operator_ref, slots_ref,
    early_buf, late_buf, stat, parts, summed, total, tables, work, left,
    in_sem, local_sem, table_send, table_recv, block_send, block_recv,
    part_send, part_recv, sum_send, sum_recv,
):
    me = lax.axis_index("rows") * cores + lax.axis_index("grp")
    order = stat.shape[1]
    share = parts.shape[1]
    reducers = stat.shape[0] // share
    half = members // 2

    def device(peer):
        return (lax.div(peer, cores), lax.rem(peer, cores))

    def table_copy(k):
        peer = me ^ k
        return pltpu.make_async_remote_copy(
            table_ref.at[peer], tables.at[me], table_send.at[k], table_recv.at[k],
            device_id=device(peer), device_id_type=MESH)

    def block_copy(k):
        peer = me ^ k
        return pltpu.make_async_remote_copy(
            payload_ref.at[pl.ds(peer * per_peer, per_peer)],
            arrived_ref.at[pl.ds(me * per_peer, per_peer)],
            block_send.at[k], block_recv.at[k],
            device_id=device(peer), device_id_type=MESH)

    def part_copy(k):
        peer = me ^ k
        return pltpu.make_async_remote_copy(
            stat.at[pl.ds(pl.multiple_of(peer * share, share), share)], parts.at[me],
            part_send.at[k], part_recv.at[k],
            device_id=device(peer), device_id_type=MESH)

    def sum_copy(k):
        return pltpu.make_async_remote_copy(
            summed, total.at[pl.ds(pl.multiple_of(me * share, share), share)],
            sum_send.at[k], sum_recv.at[k],
            device_id=device(me ^ k), device_id_type=MESH)

    def each(low, high, do):
        def step(k, carry):
            do(k)
            return carry
        lax.fori_loop(low, high, step, 0)

    def offset(i):
        return (i >> 1) + half * (1 - (i & 1))

    barrier = pltpu.get_barrier_semaphore()
    each(1, members, lambda k: pl.semaphore_signal(
        barrier, inc=1, device_id=device(me ^ k), device_id_type=MESH))

    own = pl.ds(me * per_peer, per_peer)
    own_blocks = pltpu.make_async_copy(payload_ref.at[own], arrived_ref.at[own], local_sem.at[0])
    own_blocks.start()
    own_table = pltpu.make_async_copy(table_ref.at[me], tables.at[me], local_sem.at[1])
    own_table.start()

    def loads(step, slot):
        rows = pl.ds(step * chunk, chunk)
        return (
            pltpu.make_async_copy(early_ref.at[rows], early_buf.at[slot], in_sem.at[slot, 0]),
            pltpu.make_async_copy(late_ref.at[rows], late_buf.at[slot], in_sem.at[slot, 1]),
        )

    for load in loads(0, 0):
        load.start()

    pl.semaphore_wait(barrier, members - 1)

    block_copy(half).start()
    each(2, first, lambda i: block_copy(offset(i)).start())
    each(1, members, lambda k: table_copy(k).start())

    stat[...] = jnp.zeros_like(stat)
    steps = early_ref.shape[0] // chunk

    def gram_step(step, carry):
        slot = step % 2

        @pl.when(step + 1 < steps)
        def _():
            for load in loads(step + 1, 1 - slot):
                load.start()

        for load in loads(step, slot):
            load.wait()
        early = early_buf[slot].reshape((-1, order))
        late = late_buf[slot].reshape((-1, order))
        contract = (((0,), (0,)), ((), ()))
        stat[0:order, :] += lax.dot_general(
            early, early, contract, precision=HIGHEST, preferred_element_type=jnp.float32)
        stat[order:2 * order, :] += lax.dot_general(
            early, late, contract, precision=HIGHEST, preferred_element_type=jnp.float32)
        return carry

    lax.fori_loop(0, steps, gram_step, 0)

    def to_reducers(k):
        @pl.when((me ^ k) < reducers)
        def _():
            part_copy(k).start()

    each(1, members, to_reducers)
    each(first, second, lambda i: block_copy(offset(i)).start())

    @pl.when(me < reducers)
    def _():
        mine = pl.ds(pl.multiple_of(me * share, share), share)
        parts[me] = stat[mine, :]
        each(1, members, lambda k: part_copy(k).wait_recv())
        summed[...] = jnp.sum(parts[...], axis=0) / row_total
        total[mine, :] = summed[...]
        each(1, members, lambda k: sum_copy(k).start())

    each(second, members, lambda i: block_copy(offset(i)).start())

    def from_reducers(k):
        @pl.when((me ^ k) < reducers)
        def _():
            part_copy(k).wait_send()
            sum_copy(k).wait_recv()

    each(1, members, from_reducers)

    work[...] = total[0:order, :]
    row_index = lax.broadcasted_iota(jnp.int32, (order, order), 0)
    lane_index = lax.broadcasted_iota(jnp.int32, (order, order), 1)
    left[...] = (row_index == lane_index).astype(jnp.float32)

    def eliminate(j, carry):
        square = work[...]
        row = work[pl.ds(j, 1), :]
        left_row = left[pl.ds(j, 1), :]
        picked = lane_index == j
        column = jnp.sum(jnp.where(picked, square, 0.0), axis=1, keepdims=True)
        pivot = jnp.sum(jnp.where(picked[0:1, :], row, 0.0), axis=1, keepdims=True)
        scale = jnp.where(row_index[:, 0:1] > j, column / pivot, 0.0)
        work[...] = square - scale * row
        left[...] = left[...] - scale * left_row
        return carry

    lax.fori_loop(0, order, eliminate, 0)
    diagonal = jnp.sum(jnp.where(row_index == lane_index, work[...], 0.0), axis=1, keepdims=True)
    lower = left[...] / jnp.sqrt(diagonal)
    inverse = lower.T
    inverse_ref[...] = inverse
    coupled = jnp.dot(total[order:2 * order, :], inverse, precision=HIGHEST, preferred_element_type=jnp.float32)
    operator_ref[...] = jnp.dot(lower, coupled, precision=HIGHEST, preferred_element_type=jnp.float32)

    @pl.when(me < reducers)
    def _():
        each(1, members, lambda k: sum_copy(k).wait_send())

    own_table.wait()
    each(1, members, lambda k: table_copy(k).wait())
    slots_ref[...] = jnp.sum(tables[...], axis=0).astype(jnp.int32)
    own_blocks.wait()
    each(1, members, lambda k: block_copy(k).wait())


def exchange(early, late, payload, table, members, cores, per_peer, row_total):
    order = early.shape[-1]
    chunk = math.gcd(early.shape[0], 8)
    share = max(TILE, 2 * order // members)
    first = max(2, members * 12 // 32)
    second = max(first, members * 22 // 32)
    sems = [pltpu.SemaphoreType.DMA((members,))] * 8
    vmem = pl.BlockSpec(memory_space=pltpu.VMEM)
    hbm = pl.BlockSpec(memory_space=pl.ANY)
    square = jax.ShapeDtypeStruct((order, order), jnp.float32)
    return pl.pallas_call(
        functools.partial(
            exchange_kernel, members, cores, per_peer, chunk, first, second, row_total),
        out_shape=[
            jax.ShapeDtypeStruct(payload.shape, payload.dtype),
            square,
            square,
            jax.ShapeDtypeStruct(table.shape[1:], jnp.int32),
        ],
        in_specs=[hbm, hbm, hbm, hbm],
        out_specs=[hbm, vmem, vmem, vmem],
        scratch_shapes=[
            pltpu.VMEM((2, chunk) + early.shape[1:], jnp.float32),
            pltpu.VMEM((2, chunk) + early.shape[1:], jnp.float32),
            pltpu.VMEM((2 * order, order), jnp.float32),
            pltpu.VMEM((members, share, order), jnp.float32),
            pltpu.VMEM((share, order), jnp.float32),
            pltpu.VMEM((2 * order, order), jnp.float32),
            pltpu.VMEM(table.shape, jnp.float32),
            pltpu.VMEM((order, order), jnp.float32),
            pltpu.VMEM((order, order), jnp.float32),
            pltpu.SemaphoreType.DMA((2, 2)),
            pltpu.SemaphoreType.DMA((2,)),
        ] + sems,
        compiler_params=pltpu.CompilerParams(
            collective_id=0, has_side_effects=True, vmem_limit_bytes=32 * 1024 * 1024),
    )(early, late, payload, table)


def settle_kernel(group, slots_ref, arrived_ref, inverse_ref, modes_ref, held, sems):
    step = pl.program_id(0)
    steps = pl.num_programs(0)

    @pl.when(step == 0)
    def _():
        def fetch(i, carry):
            index = jnp.maximum(slots_ref[0, i] - 1, 0)
            pltpu.make_async_copy(arrived_ref.at[index], held.at[i], sems.at[i // group]).start()
            return carry

        lax.fori_loop(0, steps * group, fetch, 0)

    mine = pl.ds(step * group, group)
    pltpu.make_async_copy(arrived_ref.at[pl.ds(0, group)], held.at[mine], sems.at[step]).wait()
    rows = held[mine].reshape((-1, held.shape[-1]))
    solved = jnp.dot(rows, inverse_ref[...], precision=HIGHEST, preferred_element_type=jnp.float32)
    solved = solved.reshape((group,) + held.shape[1:])
    for b in range(group):
        full = slots_ref[0, step * group + b] > 0
        modes_ref[b] = jnp.where(full, solved[b], 0.0)


def settle(slots, arrived, inverse):
    count = CAP
    group = 16
    block = arrived.shape[1:]
    return pl.pallas_call(
        functools.partial(settle_kernel, group),
        out_shape=jax.ShapeDtypeStruct((count,) + block, arrived.dtype),
        grid=(count // group,),
        in_specs=[
            pl.BlockSpec(memory_space=pltpu.SMEM),
            pl.BlockSpec(memory_space=pl.ANY),
            pl.BlockSpec(memory_space=pltpu.VMEM),
        ],
        out_specs=pl.BlockSpec((group,) + block, lambda s: (s, 0, 0)),
        scratch_shapes=[
            pltpu.VMEM((count,) + block, arrived.dtype),
            pltpu.SemaphoreType.DMA((count // group,)),
        ],
        compiler_params=pltpu.CompilerParams(vmem_limit_bytes=32 * 1024 * 1024),
    )(slots, arrived, inverse)


def body(snap_early, snap_late, block_ids, block_owner, block_slot):
    cores = lax.axis_size("grp")
    members = lax.axis_size(("rows", "grp"))
    per_peer = (CAP + members - 1) // members
    blocks = snap_early.shape[0]
    row_total = blocks * snap_early.shape[1] * members
    me = lax.axis_index(("rows", "grp"))
    labels = jnp.arange(block_owner.shape[0], dtype=jnp.int32)
    hits = block_ids[:, None] == labels[None, :]
    packed = block_owner * CAP + block_slot
    packed_here = jnp.sum(jnp.where(hits, packed[None, :], 0), axis=1)
    owner = packed_here // CAP
    slot = packed_here % CAP
    index = jnp.arange(blocks, dtype=jnp.int32)
    earlier = (owner[:, None] == owner[None, :]) & (index[None, :] < index[:, None])
    rank = jnp.sum(earlier.astype(jnp.int32), axis=1)
    place = owner * per_peer + rank
    peers = jnp.arange(members, dtype=jnp.int32)
    lanes = jnp.arange(LANES, dtype=jnp.int32)
    to_owner = (owner[None, :] == peers[:, None]).astype(jnp.float32)
    landing = (me * per_peer + rank + 1).astype(jnp.float32)
    at_slot = jnp.where(slot[:, None] == lanes[None, :], landing[:, None], 0.0)
    table = jnp.dot(to_owner, at_slot, precision=HIGHEST)
    table = jnp.pad(table[:, None, :], ((0, 0), (0, TILE - 1), (0, 0)))
    payload = arrange(place, snap_late, members * per_peer)
    arrived, inverse, operator, slots = exchange(
        snap_early, snap_late, payload, table, members, cores, per_peer, float(row_total))
    modes = settle(slots, arrived, inverse)
    return (modes, operator)


def solution(mesh):
    placed = (
        P(("rows", "grp"), None, None),
        P(("rows", "grp"), None, None),
        P(("rows", "grp")),
        P(),
        P(),
    )
    return jax.shard_map(
        body,
        mesh=mesh,
        in_specs=placed,
        out_specs=(P(("rows", "grp"), None, None), P()),
        check_vma=False,
    )
```
